32 devices in a mesh: clips: 2 (over x), lon: 16 (over z, y, core).
Axes of the slice: x: 2, y: 2, z: 4, core: 2. Of those that a mesh axis runs over, the one named last changes fastest.
Arguments:
- video_span: bfloat16 [2, 180, 128, 192], P(None, 'clips', 'lon'), parts along dimension 1, may hold values from -6 to 6
- caches: bfloat16 [3, 2, 180, 128, 192], P(None, None, 'clips', 'lon'), parts along dimension 2, may hold values from -0.25 to 1.5
- norm_gains: float32 [3, 192], replicated, may hold values from 0.5 to 1.5
- shifts: float32 [3, 192], replicated, may hold values from -0.5 to 0.5
- weights: bfloat16 [3, 5184, 192], replicated, may hold values from -0.078125 to 0.078125
- biases: float32 [3, 192], replicated, may hold values from -0.5 to 0.5
Outputs:
- encoded: bfloat16 [2, 180, 128, 192], P(None, 'clips', 'lon'), parts along dimension 1
- carried_frames: bfloat16 [3, 2, 180, 128, 192], P(None, None, 'clips', 'lon'), parts along dimension 2
The draws below stay inside these ranges and needn't reach their ends.
There are 2 independent parts, one for each index of `clips`. The reference program is written for one: setup_inputs(seed, part) draws one part's arguments, and reference() takes and returns one part's arrays. A program takes and returns all parts, laid end to end along the dimension named above; an argument that names none is the same for every part. Nothing has to cross between parts.
All inputs are finite; a program needn't handle non-finite values.
Results may differ from the reference program's by a relative error of at most 0.0031.
Values may be sent and summed in bfloat16 or wider, within the bound.
A program may use at most 192 MiB of HBM per device.

```python
import jax
import jax.numpy as jnp
from jax import lax

C = 192
GROUPS = 32
LAYERS = 3
FRAMES = 2
H_ROWS = 90
NLON = 128


def draw_video_span(key, part):
    key_base, key_offset = jax.random.split(key, 2)
    position = jnp.arange(NLON, dtype=jnp.float32) / max(NLON - 1, 1)
    base_noise = jax.random.normal(key_base, (FRAMES, H_ROWS, NLON, C), jnp.float32)
    spread = 0.6 + 0.6 * position
    offset = 0.5 * jax.random.normal(key_offset, (C,), jnp.float32)
    ramp_level = 0.3 + 0.7 * position
    tensor = base_noise * spread[None, None, :, None] + offset[None, None, None, :] * ramp_level[None, None, :, None]
    return jnp.clip(tensor, -6.0, 6.0).astype(jnp.bfloat16)


def shard_levels(own_key, extent, cuts, smallest, top_value):
    loudness = 1.0
    for dim, parts in cuts:
        heights = jax.random.uniform(jax.random.fold_in(jax.random.fold_in(own_key, 6), dim), (parts,), jnp.float32, smallest / len(cuts), top_value / len(cuts))
        loudness = loudness * jnp.repeat(jnp.exp(heights), extent[dim] // parts).reshape((-1,) + (1,) * (len(extent) - 1 - dim))
    return loudness


def scatter_about(stream_key, dims, scale, bound, held_as=jnp.bfloat16):
    values = jax.random.normal(stream_key, dims, jnp.float32) * scale
    return jnp.minimum(jnp.maximum(values, -bound), bound).astype(held_as)


def setup_inputs(seed: int = 0, part: int = 0) -> dict:
    key_of = jax.random.split(jax.random.key(seed), 7)
    part_keys = jax.random.split(jax.random.fold_in(key_of[6], part), 7)
    return {
        "video_span": draw_video_span(jax.random.fold_in(jax.random.fold_in(key_of[6], part), 71), part),
        "caches": jnp.clip(-0.25 + 1.75 * jax.random.uniform(part_keys[1], (LAYERS, 2, H_ROWS, NLON, C), jnp.float32) ** shard_levels(part_keys[1], (LAYERS, 2, H_ROWS, NLON, C), ((3, 16),), -0.2, 0.2), -0.25, 1.5).astype(jnp.bfloat16),
        "norm_gains": jnp.clip(jax.random.uniform(key_of[2], (LAYERS, C), jnp.float32, 0.5, 1.5), 0.5, 1.5),
        "shifts": jnp.clip(jax.random.uniform(key_of[3], (LAYERS, C), jnp.float32, -0.5, 0.5), -0.5, 0.5),
        "weights": scatter_about(key_of[4], (LAYERS, 27 * C, C), (27 * C) ** -0.5, 0.078125),
        "biases": jnp.clip(jax.random.uniform(key_of[5], (LAYERS, C), jnp.float32, -0.5, 0.5), -0.5, 0.5),
    }


epsilon = 1e-06

def activate(tensor, norm_gain, norm_shift):
    members = tensor.shape[-1] // GROUPS
    grouped = tensor.reshape(tensor.shape[:-1] + (GROUPS, members))
    average = lax.optimization_barrier(jnp.mean(grouped, axis=(0, 1, 2, 4), keepdims=True))
    centered = grouped - average
    variance = lax.optimization_barrier(jnp.mean(centered * centered, axis=(0, 1, 2, 4), keepdims=True))
    normed = (centered * lax.rsqrt(variance + epsilon)).reshape(tensor.shape)
    return jax.nn.silu(normed * norm_gain + norm_shift).astype(jnp.bfloat16)

def convolve(padded, kernel, offset):
    frames_out = padded.shape[0] - 2
    lat_rows = padded.shape[1] - 2
    columns = padded.shape[2] - 2
    channels = padded.shape[3]
    accumulated = jnp.zeros((frames_out, lat_rows, columns, channels), jnp.float32)
    for tap_index in range(27):
        step_t = tap_index // 9
        step_h = tap_index // 3 % 3
        step_w = tap_index % 3
        window = padded[step_t:step_t + frames_out, step_h:step_h + lat_rows, step_w:step_w + columns]
        product = jnp.dot(window.reshape(-1, channels), kernel[tap_index * channels:(tap_index + 1) * channels], preferred_element_type=jnp.float32)
        accumulated = accumulated + product.reshape(accumulated.shape)
    return accumulated + offset

def reference(video_span, caches, norm_gains, shifts, weights, biases):
    source = video_span.astype(jnp.float32)
    carried = []

    def apply_section(tensor, section_index):
        activation = activate(tensor, norm_gains[section_index], shifts[section_index])
        joined = jnp.concatenate([caches[section_index], activation], axis=0)
        carried.append(joined[-2:])
        padded = jnp.pad(joined, ((0, 0), (1, 1), (0, 0), (0, 0)))
        padded = jnp.concatenate([padded[:, :, -1:], padded, padded[:, :, :1]], axis=2)
        return convolve(padded, weights[section_index], biases[section_index])
    hidden_one = apply_section(source, 0)
    hidden_two = apply_section(hidden_one, 1)
    middle = source + hidden_two
    hidden_three = apply_section(middle, 2)
    return ((middle + hidden_three).astype(jnp.bfloat16), jnp.stack(carried))
```

```python
import functools

import jax
import jax.numpy as jnp
from jax import lax
from jax.experimental import pallas as pl
from jax.experimental.pallas import tpu as pltpu
from jax.sharding import PartitionSpec as P

GROUPS = 32
EPSILON = 1e-06
MESH = pl.DeviceIdType.MESH
LO = 128
F32 = jnp.float32
BF16 = jnp.bfloat16


def kernel(
    peers,
    video_hbm, caches_hbm, gains_ref, shifts_ref, weights_hbm, biases_ref,
    encoded_hbm, carried_hbm,
    video, caches, weights, x, cx, acc, edge_out, edge_in, cedge_out, cedge_in,
    hx, chx, jc, ja, stat_out, stat_in, params, carried, encoded,
    in_sem, w_sem, out_sem, stat_send, stat_recv, edge_send, edge_recv, cedge_send, cedge_recv,
):
    frames, height, width, channels = video.shape
    layers = caches.shape[0]
    half = height // 2
    rows = half * 16
    total = frames * rows
    hi_width = channels - LO
    lines = total // 8
    me = lax.axis_index("lon")
    right, left = lax.rem(me + 1, peers), lax.rem(me + peers - 1, peers)
    sides = (left, right)

    video_copy = pltpu.make_async_copy(video_hbm, video, in_sem.at[0])
    video_copy.start()
    cache_copies = [
        pltpu.make_async_copy(caches_hbm.at[l], caches.at[l], in_sem.at[1 + l]) for l in range(layers)
    ]
    cache_copies[0].start()

    def weight_row(q, r, hi):
        start = (0, 640, 1152)[q]
        if not hi:
            return start + LO * r
        if r < 2:
            return start + 3 * LO + hi_width * r
        return (512, 576, 1664)[q]

    weight_copies = []
    for l in range(layers):
        copies = []
        for q in range(3):
            for r in range(3):
                for hi in range(2):
                    size = hi_width if hi else LO
                    copies.append(
                        pltpu.make_async_copy(
                            weights_hbm.at[l, :, q, r, pl.ds(LO * hi, size), :],
                            weights.at[l, :, pl.ds(weight_row(q, r, hi), size), :],
                            w_sem.at[l, len(copies)],
                        )
                    )
        weight_copies.append(copies)
    for copy in weight_copies[0]:
        copy.start()
    for l in range(1, layers):
        cache_copies[l].start()
        for copy in weight_copies[l]:
            copy.start()

    barrier = pltpu.get_barrier_semaphore()

    def greet(k, carry):
        pl.semaphore_signal(
            barrier, inc=1, device_id={"lon": lax.rem(me + k, peers)}, device_id_type=MESH
        )
        return carry

    lax.fori_loop(1, peers, greet, 0)

    params[...] = jnp.zeros_like(params)
    params[0:layers, 0:channels] = gains_ref[...]
    params[8 : 8 + layers, 0:channels] = shifts_ref[...]
    x[...] = jnp.zeros_like(x)
    cx[...] = jnp.zeros_like(cx)
    for ref in (edge_out, cedge_out):
        ref[...] = jnp.zeros_like(ref)

    group_row = lax.broadcasted_iota(jnp.int32, (2 * LO, 2 * LO), 0) // (channels // GROUPS)
    group_column = lax.broadcasted_iota(jnp.int32, (2 * LO, 2 * LO), 1) // (channels // GROUPS)
    same_group = jnp.where(group_row == group_column, 1.0, 0.0).astype(BF16)

    def spread(source, target):
        for f in range(frames):
            for hi in range(2):
                size = hi_width if hi else LO
                lanes = pl.ds(LO * hi, size)
                top = source[f, 0:half, :, lanes].astype(F32)
                bottom = source[f, half:height, :, lanes].astype(F32)
                both = jnp.concatenate([top, bottom], axis=1).reshape(rows, size)
                target[pl.ds(hi * total + f * rows, rows), 0:size] = both

    def take_edges(source, target):
        for hi in range(2):
            for side in range(2):
                column = source[pl.ds(hi * total + (width - 1) * side, lines, stride=8), :]
                target[side, hi, 0:lines, :] = column.astype(BF16)

    def edge_copies(source, target, send, recv, l):
        return [
            pltpu.make_async_remote_copy(
                src_ref=source.at[l, side],
                dst_ref=target.at[l, 1 - side],
                send_sem=send.at[l, side],
                recv_sem=recv.at[l, 1 - side],
                device_id={"lon": sides[side]},
                device_id_type=MESH,
            )
            for side in range(2)
        ]

    def local_stats(l):
        parts = []
        for hi in range(2):
            v = x[pl.ds(hi * total, total), :].reshape(lines, 8, LO)
            parts.append((jnp.sum(v, axis=0), jnp.sum(v * v, axis=0)))
        out = [
            jnp.sum(p, axis=0, keepdims=True)
            for p in (parts[0][0], parts[1][0], parts[0][1], parts[1][1])
        ]
        stat = jnp.concatenate(out + [jnp.zeros((4, LO), F32)], axis=0)
        stat_out[l] = stat
        stat_in[l, peers - 1] = stat

    def send_stats(l):
        def send(k, carry):
            pltpu.make_async_remote_copy(
                src_ref=stat_out.at[l],
                dst_ref=stat_in.at[l, k - 1],
                send_sem=stat_send.at[l],
                recv_sem=stat_recv.at[l],
                device_id={"lon": lax.rem(me + k, peers)},
                device_id_type=MESH,
            ).start()
            return carry

        lax.fori_loop(1, peers, send, 0)

    def stats_wait(sem, l):
        others = stat_in.at[l, pl.ds(0, peers - 1)]
        pltpu.make_async_copy(others, others, sem.at[l]).wait()

    def norm_terms(l):
        sums = jnp.sum(stat_in[l], axis=0)
        wide = jnp.concatenate(
            [
                jnp.concatenate([sums[0:1], sums[1:2]], axis=1),
                jnp.concatenate([sums[2:3], sums[3:4]], axis=1),
                jnp.zeros((6, 2 * LO), F32),
            ],
            axis=0,
        )
        first = wide.astype(BF16)
        rest = wide - first.astype(F32)
        second = rest.astype(BF16)
        third = (rest - second.astype(F32)).astype(BF16)
        grouped = sum(
            jnp.dot(piece, same_group, preferred_element_type=F32)
            for piece in (third, second, first)
        )
        entries = total * peers * (channels // GROUPS)
        average = grouped[0:1] / entries
        variance = jnp.maximum(grouped[1:2] / entries - average * average, 0.0)
        scale = lax.rsqrt(variance + EPSILON) * params[l : l + 1, :] * 0.5
        shift = params[8 + l : 9 + l, :] * 0.5
        return [
            tuple(t[:, LO * hi : LO * hi + LO] for t in (average, scale, shift)) for hi in range(2)
        ]

    def activate(v, terms):
        average, scale, shift = terms
        h = (v - average) * scale + shift
        return h + h * jnp.tanh(h)

    def place_edges(source, target, terms):
        for side in range(2):
            for hi in range(2):
                v = source[side, hi, 0:lines, :].astype(F32)
                if terms is not None:
                    v = activate(v, terms[hi])
                target[side, pl.ds(hi * total + (width - 1) * side, lines, stride=8), :] = v

    steps = 5 if half % 5 == 0 else 1
    size_i = half // steps
    block = size_i * 16
    column = lax.broadcasted_iota(jnp.int32, (2 * size_i, 8, LO), 1)
    lane = lax.broadcasted_iota(jnp.int32, (block, LO), 1)
    lane16 = lax.broadcasted_iota(jnp.int32, (16, LO), 1)

    def swap(v):
        return pltpu.roll(v, LO // 2, 1)

    def build(source, halo, target, terms, store):
        for f in range(frames):

            def step(s, following):
                c = steps - 1 - s
                base = f * rows + c * block
                at = pl.ds(pl.multiple_of(16 + c * block, 16), block)
                wide = []
                for hi in range(2):
                    here = pl.ds(pl.multiple_of(hi * total + base, 16), block)
                    v = source[here, :]
                    if terms is not None:
                        v = activate(v, terms[hi])
                    v3 = v.reshape(2 * size_i, 8, LO)
                    before = jnp.where(
                        column == 0,
                        halo[0, here, :].reshape(2 * size_i, 8, LO),
                        pltpu.roll(v3, 1, 1),
                    ).reshape(block, LO)
                    after = jnp.where(
                        column == width - 1,
                        halo[1, here, :].reshape(2 * size_i, 8, LO),
                        pltpu.roll(v3, width - 1, 1),
                    ).reshape(block, LO)
                    wide.append((before, v, after))
                    if store is not None:
                        size = hi_width if hi else LO
                        pair = v.reshape(size_i, 16, LO)
                        for h in range(2):
                            store[
                                f, pl.ds(h * half + c * size_i, size_i), :, LO * hi : LO * hi + size
                            ] = pair[:, 8 * h : 8 * h + 8, 0:size].astype(BF16)
                for r in range(3):
                    target[f, at, LO * r : LO * r + LO] = wide[0][r].astype(BF16)
                before, middle, after = wide[1]
                target[f, at, 384:512] = jnp.where(lane < LO // 2, before, swap(middle)).astype(BF16)
                if block > 16:
                    nexts = jnp.concatenate([after[16:], following], axis=0)
                else:
                    nexts = following
                target[f, at, 512:640] = jnp.where(lane < LO // 2, after, swap(nexts)).astype(BF16)
                return after[0:16]

            lax.fori_loop(0, steps, step, jnp.zeros((16, LO), F32))
            zeros = jnp.zeros((8, 640), F32)
            first = target[f, 16:32, :].astype(F32)
            last = target[f, rows : rows + 16, :].astype(F32)
            over = jnp.concatenate([zeros, last[0:8]], axis=0)
            under = jnp.concatenate([first[8:16], zeros], axis=0)
            target[f, rows + 16 : rows + 32, :] = under.astype(BF16)
            target[f, 0:16, 0:512] = over[:, 0:512].astype(BF16)
            target[f, 0:16, 512:640] = jnp.where(
                lane16 < LO // 2, over[:, 512:640], swap(first[:, 512:640])
            ).astype(BF16)
            target[f, rows : rows + 16, 512:640] = jnp.where(
                lane16 < LO // 2, last[:, 512:640], swap(under[:, 512:640])
            ).astype(BF16)

    def conv(source, f, l, p):
        taps = jnp.concatenate(
            [
                source[f, 0:rows, 0:640],
                source[f, 16 : 16 + rows, 0:512],
                source[f, 32 : 32 + rows, 0:576],
            ],
            axis=1,
        )
        return jnp.dot(taps, weights[l, p], preferred_element_type=F32)

    video_copy.wait()
    spread(video, x)
    local_stats(0)
    take_edges(x, edge_out.at[0])
    pl.semaphore_wait(barrier, peers - 1)
    pending = []
    send_stats(0)
    halo = edge_copies(edge_out, edge_in, edge_send, edge_recv, 0)
    for copy in halo:
        copy.start()

    cache_halos = []

    def send_cache(l):
        cache_copies[l].wait()
        spread(caches.at[l], cx.at[l])
        take_edges(cx.at[l], cedge_out.at[l])
        copies = edge_copies(cedge_out, cedge_in, cedge_send, cedge_recv, l)
        for copy in copies:
            copy.start()
        cache_halos.append(copies)

    send_cache(0)

    for l in range(layers):
        if l + 1 < layers:
            send_cache(l + 1)
        for copy in cache_halos[l]:
            copy.wait()
        place_edges(cedge_in.at[l], chx, None)
        build(cx.at[l], chx, jc, None, None)
        for copy in weight_copies[l]:
            copy.wait()
        bias = biases_ref[l : l + 1, :]
        acc[0:rows, :] = conv(jc, 0, l, 0) + bias
        acc[0:rows, :] += conv(jc, 1, l, 1)
        acc[rows:total, :] = conv(jc, 1, l, 0) + bias
        stats_wait(stat_recv, l)
        terms = norm_terms(l)
        for copy in halo:
            copy.wait()
        place_edges(edge_in.at[l], hx, terms)
        build(x, hx, ja, terms, carried.at[l])
        out = pltpu.make_async_copy(carried.at[l], carried_hbm.at[l], out_sem.at[l])
        out.start()
        pending.append(out)
        acc[0:rows, :] += conv(ja, 0, l, 2)
        acc[rows:total, :] += conv(ja, 0, l, 1)
        acc[rows:total, :] += conv(ja, 1, l, 2)
        if l == 0:
            for hi in range(2):
                size = hi_width if hi else LO
                x[pl.ds(hi * total, total), 0:size] = acc[:, LO * hi : LO * hi + size]
        elif l == 1:
            spread(video, x)
            for hi in range(2):
                size = hi_width if hi else LO
                x[pl.ds(hi * total, total), 0:size] += acc[:, LO * hi : LO * hi + size]
        else:
            for f in range(frames):
                for hi in range(2):
                    size = hi_width if hi else LO
                    v = (
                        x[pl.ds(hi * total + f * rows, rows), 0:size]
                        + acc[f * rows : f * rows + rows, LO * hi : LO * hi + size]
                    ).reshape(half, 16, size)
                    for h in range(2):
                        encoded[
                            f, h * half : h * half + half, :, LO * hi : LO * hi + size
                        ] = v[:, 8 * h : 8 * h + 8, :].astype(BF16)
        if l + 1 < layers:
            local_stats(l + 1)
            send_stats(l + 1)
            take_edges(x, edge_out.at[l + 1])
            halo = edge_copies(edge_out, edge_in, edge_send, edge_recv, l + 1)
            for copy in halo:
                copy.start()
    out = pltpu.make_async_copy(encoded, encoded_hbm, out_sem.at[layers])
    out.start()
    pending.append(out)
    for l in range(layers):
        stats_wait(stat_send, l)
    for copy in pending:
        copy.wait()


def local(peers, video_span, caches, norm_gains, shifts, weights, biases):
    frames, height, width, channels = video_span.shape
    layers = caches.shape[0]
    weights = weights.reshape(layers, 3, 3, 3, channels, channels)
    rows = height * 8
    total = frames * rows
    lines = -(-(total // 8) // 16) * 16
    anywhere = pl.BlockSpec(memory_space=pl.ANY)
    vmem = pl.BlockSpec(memory_space=pltpu.VMEM)
    dma = pltpu.SemaphoreType.DMA
    flops = 2 * total * 27 * channels * channels * layers
    return pl.pallas_call(
        functools.partial(kernel, peers),
        out_shape=(
            jax.ShapeDtypeStruct(video_span.shape, BF16),
            jax.ShapeDtypeStruct(caches.shape, BF16),
        ),
        in_specs=[anywhere, anywhere, vmem, vmem, anywhere, vmem],
        out_specs=(anywhere, anywhere),
        scratch_shapes=[
            pltpu.VMEM(video_span.shape, BF16),
            pltpu.VMEM(caches.shape, BF16),
            pltpu.VMEM((layers, 3, 9 * channels, channels), BF16),
            pltpu.VMEM((2 * total, LO), F32),
            pltpu.VMEM((layers, 2 * total, LO), F32),
            pltpu.VMEM((total, channels), F32),
            pltpu.VMEM((layers, 2, 2, lines, LO), BF16),
            pltpu.VMEM((layers, 2, 2, lines, LO), BF16),
            pltpu.VMEM((layers, 2, 2, lines, LO), BF16),
            pltpu.VMEM((layers, 2, 2, lines, LO), BF16),
            pltpu.VMEM((2, 2 * total, LO), F32),
            pltpu.VMEM((2, 2 * total, LO), F32),
            pltpu.VMEM((frames, rows + 32, 640), BF16),
            pltpu.VMEM((frames, rows + 32, 640), BF16),
            pltpu.VMEM((layers, 8, LO), F32),
            pltpu.VMEM((layers, peers, 8, LO), F32),
            pltpu.VMEM((16, 2 * LO), F32),
            pltpu.VMEM(caches.shape, BF16),
            pltpu.VMEM(video_span.shape, BF16),
            dma((1 + layers,)),
            dma((layers, 18)),
            dma((1 + layers,)),
            dma((layers,)),
            dma((layers,)),
            dma((layers, 2)),
            dma((layers, 2)),
            dma((layers, 2)),
            dma((layers, 2)),
        ],
        compiler_params=pltpu.CompilerParams(
            collective_id=0, has_side_effects=True, vmem_limit_bytes=56 * 2**20
        ),
        cost_estimate=pl.CostEstimate(
            flops=flops, bytes_accessed=20 * 2**20, transcendentals=layers * total * channels
        ),
    )(video_span, caches, norm_gains, shifts, weights, biases)


def solution(mesh):
    return jax.shard_map(
        functools.partial(local, mesh.shape["lon"]),
        mesh=mesh,
        in_specs=(
            P(None, "clips", "lon", None),
            P(None, None, "clips", "lon", None),
            P(),
            P(),
            P(),
            P(),
        ),
        out_specs=(P(None, "clips", "lon", None), P(None, None, "clips", "lon", None)),
        check_vma=False,
    )
```

```python
import functools

import jax
import jax.numpy as jnp
from jax import lax
from jax.experimental import pallas as pl
from jax.experimental.pallas import tpu as pltpu
from jax.sharding import PartitionSpec as P

GROUPS = 32
EPSILON = 1e-06
MESH = pl.DeviceIdType.MESH
LO = 128
F32 = jnp.float32
BF16 = jnp.bfloat16


def kernel(
    peers,
    video_hbm, caches_hbm, gains_ref, shifts_ref, weights_hbm, biases_ref,
    encoded_hbm, carried_hbm,
    video, caches, raw, weights, x, cx, acc, edge_out, edge_in, cedge_out, cedge_in,
    hx, chx, jc, ja, stat_out, stat_in, params, carried, encoded,
    in_sem, w_sem, out_sem, stat_send, stat_recv, edge_send, edge_recv, cedge_send, cedge_recv,
):
    frames, height, width, channels = video.shape
    layers = caches.shape[0]
    half = height // 2
    rows = half * 16
    total = frames * rows
    hi_width = channels - LO
    lines = total // 8
    me = lax.axis_index("lon")
    right, left = lax.rem(me + 1, peers), lax.rem(me + peers - 1, peers)
    sides = (left, right)

    video_copy = pltpu.make_async_copy(video_hbm, video, in_sem.at[0])
    video_copy.start()
    cache_copies = [
        pltpu.make_async_copy(caches_hbm.at[l], caches.at[l], in_sem.at[1 + l]) for l in range(layers)
    ]
    cache_copies[0].start()

    weight_copies = [
        pltpu.make_async_copy(weights_hbm.at[l], raw.at[l], w_sem.at[l]) for l in range(layers)
    ]
    weight_copies[0].start()
    for l in range(1, layers):
        cache_copies[l].start()
        weight_copies[l].start()

    barrier = pltpu.get_barrier_semaphore()

    def greet(k, carry):
        pl.semaphore_signal(
            barrier, inc=1, device_id={"lon": lax.rem(me + k, peers)}, device_id_type=MESH
        )
        return carry

    lax.fori_loop(1, peers, greet, 0)

    params[...] = jnp.zeros_like(params)
    params[0:layers, 0:channels] = gains_ref[...]
    params[8 : 8 + layers, 0:channels] = shifts_ref[...]

    group_row = lax.broadcasted_iota(jnp.int32, (2 * LO, 2 * LO), 0) // (channels // GROUPS)
    group_column = lax.broadcasted_iota(jnp.int32, (2 * LO, 2 * LO), 1) // (channels // GROUPS)
    same_group = jnp.where(group_row == group_column, 1.0, 0.0).astype(BF16)

    lane8 = lax.broadcasted_iota(jnp.int32, (8, LO), 1)

    order = []
    for q in range(3):
        tap = [9 * q + 3 * r for r in range(3)]
        for r in range(3):
            order += [tap[r], tap[r] + 1]
        order += [tap[0] + 2, tap[1] + 2]
        if q != 1:
            order.append(tap[2] + 2)
        if q == 0:
            order.append(9 + 6 + 2)
    unit = LO // 2
    lane_w = lax.broadcasted_iota(jnp.int32, (channels, LO), 1)

    def arrange(l):
        def piece(u, upper):
            tile = raw[l, :, LO * (u // 2) : LO * (u // 2) + LO].astype(F32)
            return tile if u % 2 == upper else pltpu.roll(tile, unit, 1)

        for p in range(3):
            for d in range(0, 26, 2):
                a, b = 27 * p + order[d], 27 * p + order[d + 1]
                if a % 2 == 0 and b == a + 1:
                    weights[l, p, :, unit * d : unit * d + LO] = raw[l, :, unit * a : unit * a + LO]
                else:
                    both = jnp.where(lane_w < unit, piece(a, 0), piece(b, 1))
                    weights[l, p, :, unit * d : unit * d + LO] = both.astype(BF16)
            a = 27 * p + order[26]
            if a % 2 == 0:
                weights[l, p, :, unit * 26 : unit * 27] = raw[l, :, unit * a : unit * a + unit]
            else:
                weights[l, p, :, unit * 26 : unit * 27] = piece(a, 0)[:, 0:unit].astype(BF16)

    def spread(source, target):
        for f in range(frames):
            for hi in range(2):
                size = hi_width if hi else LO
                lanes = pl.ds(LO * hi, size)
                top = source[f, 0:half, :, lanes].astype(F32)
                bottom = source[f, half:height, :, lanes].astype(F32)
                both = jnp.concatenate([top, bottom], axis=1).reshape(rows, size)
                target[pl.ds(hi * total + f * rows, rows), 0:size] = both

    def take_edges(source, target):
        for hi in range(2):
            for side in range(2):
                column = source[pl.ds(hi * total + (width - 1) * side, lines, stride=8), :]
                target[side, hi, 0:lines, :] = column.astype(BF16)

    def edge_copies(source, target, send, recv, l):
        return [
            pltpu.make_async_remote_copy(
                src_ref=source.at[l, side],
                dst_ref=target.at[l, 1 - side],
                send_sem=send.at[l, side],
                recv_sem=recv.at[l, 1 - side],
                device_id={"lon": sides[side]},
                device_id_type=MESH,
            )
            for side in range(2)
        ]

    def local_stats(l):
        parts = []
        for hi in range(2):
            v = x[pl.ds(hi * total, total), :].reshape(lines, 8, LO)
            sums = (jnp.sum(v, axis=0), jnp.sum(v * v, axis=0))
            if hi:
                sums = tuple(jnp.where(lane8 < hi_width, t, 0.0) for t in sums)
            parts.append(sums)
        out = [
            jnp.sum(p, axis=0, keepdims=True)
            for p in (parts[0][0], parts[1][0], parts[0][1], parts[1][1])
        ]
        stat = jnp.concatenate(out + [jnp.zeros((4, LO), F32)], axis=0)
        stat_out[l] = stat
        stat_in[l, peers - 1] = stat

    def send_stats(l):
        def send(k, carry):
            pltpu.make_async_remote_copy(
                src_ref=stat_out.at[l],
                dst_ref=stat_in.at[l, k - 1],
                send_sem=stat_send.at[l],
                recv_sem=stat_recv.at[l],
                device_id={"lon": lax.rem(me + k, peers)},
                device_id_type=MESH,
            ).start()
            return carry

        lax.fori_loop(1, peers, send, 0)

    def stats_wait(sem, l):
        others = stat_in.at[l, pl.ds(0, peers - 1)]
        pltpu.make_async_copy(others, others, sem.at[l]).wait()

    def norm_terms(l):
        sums = jnp.sum(stat_in[l], axis=0)
        wide = jnp.concatenate(
            [
                jnp.concatenate([sums[0:1], sums[1:2]], axis=1),
                jnp.concatenate([sums[2:3], sums[3:4]], axis=1),
                jnp.zeros((6, 2 * LO), F32),
            ],
            axis=0,
        )
        first = wide.astype(BF16)
        rest = wide - first.astype(F32)
        second = rest.astype(BF16)
        third = (rest - second.astype(F32)).astype(BF16)
        grouped = sum(
            jnp.dot(piece, same_group, preferred_element_type=F32)
            for piece in (third, second, first)
        )
        entries = total * peers * (channels // GROUPS)
        average = grouped[0:1] / entries
        variance = jnp.maximum(grouped[1:2] / entries - average * average, 0.0)
        scale = lax.rsqrt(variance + EPSILON) * params[l : l + 1, :] * 0.5
        shift = params[8 + l : 9 + l, :] * 0.5
        return [
            tuple(t[:, LO * hi : LO * hi + LO] for t in (average, scale, shift)) for hi in range(2)
        ]

    def activate(v, terms):
        average, scale, shift = terms
        h = (v - average) * scale + shift
        return h + h * jnp.tanh(h)

    def place_edges(source, target, terms):
        for side in range(2):
            for hi in range(2):
                v = source[side, hi, 0:lines, :].astype(F32)
                if terms is not None:
                    v = activate(v, terms[hi])
                target[side, pl.ds(hi * total + (width - 1) * side, lines, stride=8), :] = v

    steps = 5 if half % 5 == 0 else 1
    size_i = half // steps
    block = size_i * 16
    column = lax.broadcasted_iota(jnp.int32, (2 * size_i, 8, LO), 1)
    lane = lax.broadcasted_iota(jnp.int32, (block, LO), 1)
    lane16 = lax.broadcasted_iota(jnp.int32, (16, LO), 1)

    def swap(v):
        return pltpu.roll(v, LO // 2, 1)

    def build(source, halo, target, terms, store, only):
        for f in only:

            def step(s, following):
                c = steps - 1 - s
                base = f * rows + c * block
                at = pl.ds(16 + c * block, block)
                wide = []
                for hi in range(2):
                    here = pl.ds(hi * total + base, block)
                    v = source[here, :]
                    if terms is not None:
                        v = activate(v, terms[hi])
                    v3 = v.reshape(2 * size_i, 8, LO)
                    before = jnp.where(
                        column == 0,
                        halo[0, here, :].reshape(2 * size_i, 8, LO),
                        pltpu.roll(v3, 1, 1),
                    ).reshape(block, LO)
                    after = jnp.where(
                        column == width - 1,
                        halo[1, here, :].reshape(2 * size_i, 8, LO),
                        pltpu.roll(v3, width - 1, 1),
                    ).reshape(block, LO)
                    wide.append((before, v, after))
                    if store is not None:
                        size = hi_width if hi else LO
                        pair = v.reshape(size_i, 16, LO)
                        for h in range(2):
                            store[
                                f, pl.ds(h * half + c * size_i, size_i), :, LO * hi : LO * hi + size
                            ] = pair[:, 8 * h : 8 * h + 8, 0:size].astype(BF16)
                for r in range(3):
                    target[f, at, LO * r : LO * r + LO] = wide[0][r].astype(BF16)
                before, middle, after = wide[1]
                target[f, at, 384:512] = jnp.where(lane < LO // 2, before, swap(middle)).astype(BF16)
                if block > 16:
                    nexts = jnp.concatenate([after[16:], following], axis=0)
                else:
                    nexts = following
                target[f, at, 512:640] = jnp.where(lane < LO // 2, after, swap(nexts)).astype(BF16)
                return after[0:16]

            following = jnp.zeros((16, LO), F32)
            for s in range(steps):
                following = step(s, following)
            zeros = jnp.zeros((8, 640), F32)
            first = target[f, 16:32, :].astype(F32)
            last = target[f, rows : rows + 16, :].astype(F32)
            over = jnp.concatenate([zeros, last[0:8]], axis=0)
            under = jnp.concatenate([first[8:16], zeros], axis=0)
            target[f, rows + 16 : rows + 32, :] = under.astype(BF16)
            target[f, 0:16, 0:512] = over[:, 0:512].astype(BF16)
            target[f, 0:16, 512:640] = jnp.where(
                lane16 < LO // 2, over[:, 512:640], swap(first[:, 512:640])
            ).astype(BF16)
            target[f, rows : rows + 16, 512:640] = jnp.where(
                lane16 < LO // 2, last[:, 512:640], swap(under[:, 512:640])
            ).astype(BF16)

    def conv(source, f, l, p):
        taps = jnp.concatenate(
            [
                source[f, 0:rows, 0:640],
                source[f, 16 : 16 + rows, 0:512],
                source[f, 32 : 32 + rows, 0:576],
            ],
            axis=1,
        )
        return lax.dot_general(
            taps, weights[l, p], (((1,), (1,)), ((), ())), preferred_element_type=F32
        )

    video_copy.wait()
    spread(video, x)
    local_stats(0)
    take_edges(x, edge_out.at[0])
    pl.semaphore_wait(barrier, peers - 1)
    pending = []
    send_stats(0)
    halo = edge_copies(edge_out, edge_in, edge_send, edge_recv, 0)
    for copy in halo:
        copy.start()

    cache_halos = []

    def send_cache(l):
        cache_copies[l].wait()
        spread(caches.at[l], cx.at[l])
        take_edges(cx.at[l], cedge_out.at[l])
        copies = edge_copies(cedge_out, cedge_in, cedge_send, cedge_recv, l)
        for copy in copies:
            copy.start()
        cache_halos.append(copies)

    def build_cache(l):
        for copy in cache_halos[l]:
            copy.wait()
        place_edges(cedge_in.at[l], chx, None)
        build(cx.at[l], chx, jc, None, None, range(frames))

    for l in range(layers):
        send_cache(l)
    weight_copies[0].wait()
    arrange(0)
    build_cache(0)

    for l in range(layers):
        bias = biases_ref[l : l + 1, :]
        acc[0:rows, :] = conv(jc, 0, l, 0) + bias
        acc[0:rows, :] += conv(jc, 1, l, 1)
        acc[rows:total, :] = conv(jc, 1, l, 0) + bias
        stats_wait(stat_recv, l)
        terms = norm_terms(l)
        for copy in halo:
            copy.wait()
        place_edges(edge_in.at[l], hx, terms)
        if l + 1 < layers:
            for copy in cache_halos[l + 1]:
                copy.wait()
            weight_copies[l + 1].wait()
        build(x, hx, ja, terms, carried.at[l], (0,))
        acc[0:rows, :] += conv(ja, 0, l, 2)
        build(x, hx, ja, terms, carried.at[l], (1,))
        acc[rows:total, :] += conv(ja, 0, l, 1)
        if l + 1 < layers:
            place_edges(cedge_in.at[l + 1], chx, None)
            build(cx.at[l + 1], chx, jc, None, None, range(frames))
            arrange(l + 1)
        acc[rows:total, :] += conv(ja, 1, l, 2)
        out = pltpu.make_async_copy(carried.at[l], carried_hbm.at[l], out_sem.at[l])
        out.start()
        pending.append(out)
        if l == 0:
            for hi in range(2):
                size = hi_width if hi else LO
                x[pl.ds(hi * total, total), 0:size] = acc[:, LO * hi : LO * hi + size]
        elif l == 1:
            spread(video, x)
            for hi in range(2):
                size = hi_width if hi else LO
                x[pl.ds(hi * total, total), 0:size] += acc[:, LO * hi : LO * hi + size]
        else:
            for f in range(frames):
                for hi in range(2):
                    size = hi_width if hi else LO
                    v = (
                        x[pl.ds(hi * total + f * rows, rows), 0:size]
                        + acc[f * rows : f * rows + rows, LO * hi : LO * hi + size]
                    ).reshape(half, 16, size)
                    for h in range(2):
                        encoded[
                            f, h * half : h * half + half, :, LO * hi : LO * hi + size
                        ] = v[:, 8 * h : 8 * h + 8, :].astype(BF16)
        if l + 1 < layers:
            local_stats(l + 1)
            send_stats(l + 1)
            take_edges(x, edge_out.at[l + 1])
            halo = edge_copies(edge_out, edge_in, edge_send, edge_recv, l + 1)
            for copy in halo:
                copy.start()
    out = pltpu.make_async_copy(encoded, encoded_hbm, out_sem.at[layers])
    out.start()
    pending.append(out)
    for l in range(layers):
        stats_wait(stat_send, l)
    for copy in pending:
        copy.wait()


def hand_over(encoded, carried, encoded_out, carried_out, sem):
    layers, frames = carried.shape[:2]
    copies = []
    for f in range(frames):
        copies.append(pltpu.make_async_copy(encoded.at[f], encoded_out.at[f], sem.at[len(copies)]))
        for l in range(layers):
            copies.append(
                pltpu.make_async_copy(carried.at[l, f], carried_out.at[l, f], sem.at[len(copies)])
            )
    for copy in copies:
        copy.start()
    for copy in copies:
        copy.wait()


def local(peers, video_span, caches, norm_gains, shifts, weights, biases):
    frames, height, width, channels = video_span.shape
    layers = caches.shape[0]
    weights = jnp.swapaxes(weights, 1, 2)
    rows = height * 8
    total = frames * rows
    lines = -(-(total // 8) // 16) * 16
    anywhere = pl.BlockSpec(memory_space=pl.ANY)
    vmem = pl.BlockSpec(memory_space=pltpu.VMEM)
    dma = pltpu.SemaphoreType.DMA
    flops = 2 * total * 27 * channels * channels * layers
    encoded, carried = pl.pallas_call(
        functools.partial(kernel, peers),
        out_shape=(
            jax.ShapeDtypeStruct(video_span.shape, BF16),
            jax.ShapeDtypeStruct(caches.shape, BF16),
        ),
        in_specs=[anywhere, anywhere, vmem, vmem, anywhere, vmem],
        out_specs=(anywhere, anywhere),
        scratch_shapes=[
            pltpu.VMEM(video_span.shape, BF16),
            pltpu.VMEM(caches.shape, BF16),
            pltpu.VMEM((layers, channels, 27 * channels), BF16),
            pltpu.VMEM((layers, 3, channels, 9 * channels), BF16),
            pltpu.VMEM((2 * total, LO), F32),
            pltpu.VMEM((layers, 2 * total, LO), F32),
            pltpu.VMEM((total, channels), F32),
            pltpu.VMEM((layers, 2, 2, lines, LO), BF16),
            pltpu.VMEM((layers, 2, 2, lines, LO), BF16),
            pltpu.VMEM((layers, 2, 2, lines, LO), BF16),
            pltpu.VMEM((layers, 2, 2, lines, LO), BF16),
            pltpu.VMEM((2, 2 * total, LO), F32),
            pltpu.VMEM((2, 2 * total, LO), F32),
            pltpu.VMEM((frames, rows + 32, 640), BF16),
            pltpu.VMEM((frames, rows + 32, 640), BF16),
            pltpu.VMEM((layers, 8, LO), F32),
            pltpu.VMEM((layers, peers, 8, LO), F32),
            pltpu.VMEM((16, 2 * LO), F32),
            pltpu.VMEM(caches.shape, BF16),
            pltpu.VMEM(video_span.shape, BF16),
            dma((1 + layers,)),
            dma((layers,)),
            dma((1 + layers,)),
            dma((layers,)),
            dma((layers,)),
            dma((layers, 2)),
            dma((layers, 2)),
            dma((layers, 2)),
            dma((layers, 2)),
        ],
        compiler_params=pltpu.CompilerParams(
            collective_id=0, has_side_effects=True, vmem_limit_bytes=56 * 2**20
        ),
        cost_estimate=pl.CostEstimate(
            flops=flops, bytes_accessed=20 * 2**20, transcendentals=layers * total * channels
        ),
    )(video_span, caches, norm_gains, shifts, weights, biases)
    return pl.pallas_call(
        hand_over,
        out_shape=(
            jax.ShapeDtypeStruct(video_span.shape, BF16),
            jax.ShapeDtypeStruct(caches.shape, BF16),
        ),
        in_specs=[anywhere, anywhere],
        out_specs=(anywhere, anywhere),
        scratch_shapes=[dma(((1 + layers) * frames,))],
    )(encoded, carried)


def solution(mesh):
    return jax.shard_map(
        functools.partial(local, mesh.shape["lon"]),
        mesh=mesh,
        in_specs=(
            P(None, "clips", "lon", None),
            P(None, None, "clips", "lon", None),
            P(),
            P(),
            P(),
            P(),
        ),
        out_specs=(P(None, "clips", "lon", None), P(None, None, "clips", "lon", None)),
        check_vma=False,
    )
```

```python
import functools

import jax
import jax.numpy as jnp
from jax import lax
from jax.experimental import pallas as pl
from jax.experimental.pallas import tpu as pltpu
from jax.sharding import PartitionSpec as P

GROUPS = 32
EPSILON = 1e-06
MESH = pl.DeviceIdType.MESH
LO = 128
F32 = jnp.float32
BF16 = jnp.bfloat16


def kernel(
    peers,
    video_hbm, caches_hbm, gains_ref, shifts_ref, weights_hbm, biases_ref,
    encoded_hbm, carried_hbm,
    video, caches, raw, weights, x, cx, acc, edge_out, edge_in, cedge_out, cedge_in,
    hx, chx, jc, ja, stat_out, stat_in, params, carried, encoded,
    in_sem, w_sem, out_sem, stat_send, stat_recv, edge_send, edge_recv, cedge_send, cedge_recv,
):
    frames, height, width, channels = video.shape
    layers = caches.shape[0]
    half = height // 2
    rows = half * 16
    total = frames * rows
    hi_width = channels - LO
    lines = total // 8
    me = lax.axis_index("lon")
    right, left = lax.rem(me + 1, peers), lax.rem(me + peers - 1, peers)
    sides = (left, right)

    video_copy = pltpu.make_async_copy(video_hbm, video, in_sem.at[0])
    video_copy.start()
    cache_copies = [
        pltpu.make_async_copy(caches_hbm.at[l], caches.at[l], in_sem.at[1 + l]) for l in range(layers)
    ]
    cache_copies[0].start()

    weight_copies = [
        pltpu.make_async_copy(weights_hbm.at[l], raw.at[l], w_sem.at[l]) for l in range(layers)
    ]
    weight_copies[0].start()
    for l in range(1, layers):
        cache_copies[l].start()
        weight_copies[l].start()

    barrier = pltpu.get_barrier_semaphore()

    def greet(k, carry):
        pl.semaphore_signal(
            barrier, inc=1, device_id={"lon": lax.rem(me + k, peers)}, device_id_type=MESH
        )
        return carry

    lax.fori_loop(1, peers, greet, 0)

    params[...] = jnp.zeros_like(params)
    params[0:layers, 0:channels] = gains_ref[...]
    params[8 : 8 + layers, 0:channels] = shifts_ref[...]

    group_row = lax.broadcasted_iota(jnp.int32, (2 * LO, 2 * LO), 0) // (channels // GROUPS)
    group_column = lax.broadcasted_iota(jnp.int32, (2 * LO, 2 * LO), 1) // (channels // GROUPS)
    same_group = jnp.where(group_row == group_column, 1.0, 0.0).astype(BF16)

    lane8 = lax.broadcasted_iota(jnp.int32, (8, LO), 1)

    order = []
    for q in range(3):
        tap = [9 * q + 3 * r for r in range(3)]
        for r in range(3):
            order += [tap[r], tap[r] + 1]
        order += [tap[0] + 2, tap[1] + 2]
        if q != 1:
            order.append(tap[2] + 2)
        if q == 0:
            order.append(9 + 6 + 2)
    unit = LO // 2
    lane_w = lax.broadcasted_iota(jnp.int32, (channels, LO), 1)

    def arrange(l):
        def piece(u, upper):
            tile = raw[l, :, LO * (u // 2) : LO * (u // 2) + LO].astype(F32)
            return tile if u % 2 == upper else pltpu.roll(tile, unit, 1)

        for p in range(3):
            for d in range(0, 26, 2):
                a, b = 27 * p + order[d], 27 * p + order[d + 1]
                if a % 2 == 0 and b == a + 1:
                    weights[l, p, :, unit * d : unit * d + LO] = raw[l, :, unit * a : unit * a + LO]
                else:
                    both = jnp.where(lane_w < unit, piece(a, 0), piece(b, 1))
                    weights[l, p, :, unit * d : unit * d + LO] = both.astype(BF16)
            a = 27 * p + order[26]
            if a % 2 == 0:
                weights[l, p, :, unit * 26 : unit * 27] = raw[l, :, unit * a : unit * a + unit]
            else:
                weights[l, p, :, unit * 26 : unit * 27] = piece(a, 0)[:, 0:unit].astype(BF16)

    def spread(source, target):
        for f in range(frames):
            for hi in range(2):
                size = hi_width if hi else LO
                lanes = pl.ds(LO * hi, size)
                top = source[f, 0:half, :, lanes].astype(F32)
                bottom = source[f, half:height, :, lanes].astype(F32)
                both = jnp.concatenate([top, bottom], axis=1).reshape(rows, size)
                target[pl.ds(hi * total + f * rows, rows), 0:size] = both

    def take_edges(source, target):
        for hi in range(2):
            for side in range(2):
                column = source[pl.ds(hi * total + (width - 1) * side, lines, stride=8), :]
                target[side, hi, 0:lines, :] = column.astype(BF16)

    def edge_copies(source, target, send, recv, l):
        return [
            pltpu.make_async_remote_copy(
                src_ref=source.at[l, side],
                dst_ref=target.at[l, 1 - side],
                send_sem=send.at[l, side],
                recv_sem=recv.at[l, 1 - side],
                device_id={"lon": sides[side]},
                device_id_type=MESH,
            )
            for side in range(2)
        ]

    def local_stats(l):
        parts = []
        for hi in range(2):
            v = x[pl.ds(hi * total, total), :].reshape(lines, 8, LO)
            sums = (jnp.sum(v, axis=0), jnp.sum(v * v, axis=0))
            if hi:
                sums = tuple(jnp.where(lane8 < hi_width, t, 0.0) for t in sums)
            parts.append(sums)
        out = [
            jnp.sum(p, axis=0, keepdims=True)
            for p in (parts[0][0], parts[1][0], parts[0][1], parts[1][1])
        ]
        stat = jnp.concatenate(out + [jnp.zeros((4, LO), F32)], axis=0)
        stat_out[l] = stat
        stat_in[l, peers - 1] = stat

    def send_stats(l):
        def send(k, carry):
            pltpu.make_async_remote_copy(
                src_ref=stat_out.at[l],
                dst_ref=stat_in.at[l, k - 1],
                send_sem=stat_send.at[l],
                recv_sem=stat_recv.at[l],
                device_id={"lon": lax.rem(me + k, peers)},
                device_id_type=MESH,
            ).start()
            return carry

        lax.fori_loop(1, peers, send, 0)

    def stats_wait(sem, l):
        others = stat_in.at[l, pl.ds(0, peers - 1)]
        pltpu.make_async_copy(others, others, sem.at[l]).wait()

    def norm_terms(l):
        sums = jnp.sum(stat_in[l], axis=0)
        wide = jnp.concatenate(
            [
                jnp.concatenate([sums[0:1], sums[1:2]], axis=1),
                jnp.concatenate([sums[2:3], sums[3:4]], axis=1),
                jnp.zeros((6, 2 * LO), F32),
            ],
            axis=0,
        )
        first = wide.astype(BF16).astype(F32)
        second = (wide - first).astype(BF16).astype(F32)
        third = wide - first - second
        pieces = jnp.concatenate([third, second, first], axis=0).astype(BF16)
        grouped = jnp.dot(pieces, same_group, preferred_element_type=F32)
        grouped = grouped[0:8] + grouped[8:16] + grouped[16:24]
        entries = total * peers * (channels // GROUPS)
        average = grouped[0:1] / entries
        variance = jnp.maximum(grouped[1:2] / entries - average * average, 0.0)
        scale = lax.rsqrt(variance + EPSILON) * params[l : l + 1, :] * 0.5
        shift = params[8 + l : 9 + l, :] * 0.5
        return [
            tuple(t[:, LO * hi : LO * hi + LO] for t in (average, scale, shift)) for hi in range(2)
        ]

    def activate(v, terms):
        average, scale, shift = terms
        h = (v - average) * scale + shift
        return h + h * jnp.tanh(h)

    def place_edges(source, target, terms):
        for side in range(2):
            for hi in range(2):
                v = source[side, hi, 0:lines, :].astype(F32)
                if terms is not None:
                    v = activate(v, terms[hi])
                target[side, pl.ds(hi * total + (width - 1) * side, lines, stride=8), :] = v

    steps = 5 if half % 5 == 0 else 1
    size_i = half // steps
    block = size_i * 16
    column = lax.broadcasted_iota(jnp.int32, (2 * size_i, 8, LO), 1)
    lane = lax.broadcasted_iota(jnp.int32, (block, LO), 1)
    lane16 = lax.broadcasted_iota(jnp.int32, (16, LO), 1)

    def swap(v):
        return pltpu.roll(v, LO // 2, 1)

    def build(source, halo, target, terms, store, only):
        for f in only:

            def step(s, following):
                c = steps - 1 - s
                base = f * rows + c * block
                at = pl.ds(16 + c * block, block)
                wide = []
                for hi in range(2):
                    here = pl.ds(hi * total + base, block)
                    v = source[here, :]
                    if terms is not None:
                        v = activate(v, terms[hi])
                    v3 = v.reshape(2 * size_i, 8, LO)
                    before = jnp.where(
                        column == 0,
                        halo[0, here, :].reshape(2 * size_i, 8, LO),
                        pltpu.roll(v3, 1, 1),
                    ).reshape(block, LO)
                    after = jnp.where(
                        column == width - 1,
                        halo[1, here, :].reshape(2 * size_i, 8, LO),
                        pltpu.roll(v3, width - 1, 1),
                    ).reshape(block, LO)
                    wide.append((before, v, after))
                    if store is not None:
                        size = hi_width if hi else LO
                        pair = v.reshape(size_i, 16, LO)
                        for h in range(2):
                            store[
                                f, pl.ds(h * half + c * size_i, size_i), :, LO * hi : LO * hi + size
                            ] = pair[:, 8 * h : 8 * h + 8, 0:size].astype(BF16)
                for r in range(3):
                    target[f, at, LO * r : LO * r + LO] = wide[0][r].astype(BF16)
                before, middle, after = wide[1]
                target[f, at, 384:512] = jnp.where(lane < LO // 2, before, swap(middle)).astype(BF16)
                if block > 16:
                    nexts = jnp.concatenate([after[16:], following], axis=0)
                else:
                    nexts = following
                target[f, at, 512:640] = jnp.where(lane < LO // 2, after, swap(nexts)).astype(BF16)
                return after[0:16]

            following = jnp.zeros((16, LO), F32)
            for s in range(steps):
                following = step(s, following)
            zeros = jnp.zeros((8, 640), F32)
            first = target[f, 16:32, :].astype(F32)
            last = target[f, rows : rows + 16, :].astype(F32)
            over = jnp.concatenate([zeros, last[0:8]], axis=0)
            under = jnp.concatenate([first[8:16], zeros], axis=0)
            target[f, rows + 16 : rows + 32, :] = under.astype(BF16)
            target[f, 0:16, 0:512] = over[:, 0:512].astype(BF16)
            target[f, 0:16, 512:640] = jnp.where(
                lane16 < LO // 2, over[:, 512:640], swap(first[:, 512:640])
            ).astype(BF16)
            target[f, rows : rows + 16, 512:640] = jnp.where(
                lane16 < LO // 2, last[:, 512:640], swap(under[:, 512:640])
            ).astype(BF16)

    def conv(source, which, l, p):
        taps = jnp.concatenate(
            [
                jnp.concatenate(
                    [
                        source[f, 0:rows, 0:640],
                        source[f, 16 : 16 + rows, 0:512],
                        source[f, 32 : 32 + rows, 0:576],
                    ],
                    axis=1,
                )
                for f in which
            ],
            axis=0,
        )
        return lax.dot_general(
            taps, weights[l, p], (((1,), (1,)), ((), ())), preferred_element_type=F32
        )

    video_copy.wait()
    spread(video, x)
    local_stats(0)
    take_edges(x, edge_out.at[0])
    pl.semaphore_wait(barrier, peers - 1)
    pending = []
    send_stats(0)
    halo = edge_copies(edge_out, edge_in, edge_send, edge_recv, 0)
    for copy in halo:
        copy.start()

    cache_halos = [
        edge_copies(cedge_out, cedge_in, cedge_send, cedge_recv, l) for l in range(layers)
    ]

    def prepare_cache(l):
        spread(caches.at[l], cx.at[l])
        take_edges(cx.at[l], cedge_out.at[l])

    def build_cache(l):
        place_edges(cedge_in.at[l], chx, None)
        build(cx.at[l], chx, jc.at[l % 2], None, None, range(frames))

    cache_copies[0].wait()
    prepare_cache(0)
    for copy in cache_halos[0]:
        copy.start()
    weight_copies[0].wait()
    arrange(0)
    for copy in cache_halos[0]:
        copy.wait()
    build_cache(0)

    for l in range(layers):
        if l == 0:
            for later in range(1, layers):
                cache_copies[later].wait()
        elif l + 1 < layers:
            for copy in cache_halos[l + 1]:
                copy.wait()
        if l + 1 < layers:
            weight_copies[l + 1].wait()
        now = jc.at[l % 2]
        acc[...] = conv(now, (0, 1), l, 0) + biases_ref[l : l + 1, :]
        if l == 0:
            for later in range(1, layers):
                prepare_cache(later)
        elif l + 1 < layers:
            build_cache(l + 1)
        if l + 1 < layers:
            arrange(l + 1)
        acc[0:rows, :] += conv(now, (1,), l, 1)
        if l == 0:
            for later in range(1, layers):
                for copy in cache_halos[later]:
                    copy.start()
        stats_wait(stat_recv, l)
        terms = norm_terms(l)
        for copy in halo:
            copy.wait()
        place_edges(edge_in.at[l], hx, terms)
        build(x, hx, ja, terms, carried.at[l], (0,))
        acc[0:rows, :] += conv(ja, (0,), l, 2)
        build(x, hx, ja, terms, carried.at[l], (1,))
        acc[rows:total, :] += conv(ja, (0,), l, 1)
        if l == 0 and l + 1 < layers:
            for copy in cache_halos[1]:
                copy.wait()
            build_cache(1)
        acc[rows:total, :] += conv(ja, (1,), l, 2)
        out = pltpu.make_async_copy(carried.at[l], carried_hbm.at[l], out_sem.at[l])
        out.start()
        pending.append(out)
        if l == 0:
            for hi in range(2):
                size = hi_width if hi else LO
                x[pl.ds(hi * total, total), 0:size] = acc[:, LO * hi : LO * hi + size]
        elif l == 1:
            spread(video, x)
            for hi in range(2):
                size = hi_width if hi else LO
                x[pl.ds(hi * total, total), 0:size] += acc[:, LO * hi : LO * hi + size]
        else:
            for f in range(frames):
                for hi in range(2):
                    size = hi_width if hi else LO
                    v = (
                        x[pl.ds(hi * total + f * rows, rows), 0:size]
                        + acc[f * rows : f * rows + rows, LO * hi : LO * hi + size]
                    ).reshape(half, 16, size)
                    for h in range(2):
                        encoded[
                            f, h * half : h * half + half, :, LO * hi : LO * hi + size
                        ] = v[:, 8 * h : 8 * h + 8, :].astype(BF16)
        if l + 1 < layers:
            local_stats(l + 1)
            send_stats(l + 1)
            take_edges(x, edge_out.at[l + 1])
            halo = edge_copies(edge_out, edge_in, edge_send, edge_recv, l + 1)
            for copy in halo:
                copy.start()
    out = pltpu.make_async_copy(encoded, encoded_hbm, out_sem.at[layers])
    out.start()
    pending.append(out)
    for l in range(layers):
        stats_wait(stat_send, l)
    for copy in pending:
        copy.wait()


def hand_over(encoded, carried, encoded_out, carried_out, held, held_all, in_sem, out_sem):
    layers, frames = carried.shape[:2]
    parts = []
    for f in range(frames):
        parts.append((encoded.at[f], held.at[f], encoded_out.at[f]))
        for l in range(layers):
            parts.append((carried.at[l, f], held_all.at[l, f], carried_out.at[l, f]))
    ins = [pltpu.make_async_copy(a, b, in_sem.at[i]) for i, (a, b, _) in enumerate(parts)]
    outs = [pltpu.make_async_copy(b, c, out_sem.at[i]) for i, (_, b, c) in enumerate(parts)]
    for copy in ins:
        copy.start()
    for arrive, leave in zip(ins, outs):
        arrive.wait()
        leave.start()
    for copy in outs:
        copy.wait()


def local(peers, video_span, caches, norm_gains, shifts, weights, biases):
    frames, height, width, channels = video_span.shape
    layers = caches.shape[0]
    weights = jnp.swapaxes(weights, 1, 2)
    rows = height * 8
    total = frames * rows
    lines = -(-(total // 8) // 16) * 16
    anywhere = pl.BlockSpec(memory_space=pl.ANY)
    vmem = pl.BlockSpec(memory_space=pltpu.VMEM)
    dma = pltpu.SemaphoreType.DMA
    flops = 2 * total * 27 * channels * channels * layers
    encoded, carried = pl.pallas_call(
        functools.partial(kernel, peers),
        out_shape=(
            jax.ShapeDtypeStruct(video_span.shape, BF16),
            jax.ShapeDtypeStruct(caches.shape, BF16),
        ),
        in_specs=[anywhere, anywhere, vmem, vmem, anywhere, vmem],
        out_specs=(anywhere, anywhere),
        scratch_shapes=[
            pltpu.VMEM(video_span.shape, BF16),
            pltpu.VMEM(caches.shape, BF16),
            pltpu.VMEM((layers, channels, 27 * channels), BF16),
            pltpu.VMEM((layers, 3, channels, 9 * channels), BF16),
            pltpu.VMEM((2 * total, LO), F32),
            pltpu.VMEM((layers, 2 * total, LO), F32),
            pltpu.VMEM((total, channels), F32),
            pltpu.VMEM((layers, 2, 2, lines, LO), BF16),
            pltpu.VMEM((layers, 2, 2, lines, LO), BF16),
            pltpu.VMEM((layers, 2, 2, lines, LO), BF16),
            pltpu.VMEM((layers, 2, 2, lines, LO), BF16),
            pltpu.VMEM((2, 2 * total, LO), F32),
            pltpu.VMEM((2, 2 * total, LO), F32),
            pltpu.VMEM((2, frames, rows + 32, 640), BF16),
            pltpu.VMEM((frames, rows + 32, 640), BF16),
            pltpu.VMEM((layers, 8, LO), F32),
            pltpu.VMEM((layers, peers, 8, LO), F32),
            pltpu.VMEM((16, 2 * LO), F32),
            pltpu.VMEM(caches.shape, BF16),
            pltpu.VMEM(video_span.shape, BF16),
            dma((1 + layers,)),
            dma((layers,)),
            dma((1 + layers,)),
            dma((layers,)),
            dma((layers,)),
            dma((layers, 2)),
            dma((layers, 2)),
            dma((layers, 2)),
            dma((layers, 2)),
        ],
        compiler_params=pltpu.CompilerParams(
            collective_id=0, has_side_effects=True, vmem_limit_bytes=56 * 2**20
        ),
        cost_estimate=pl.CostEstimate(
            flops=flops, bytes_accessed=20 * 2**20, transcendentals=layers * total * channels
        ),
    )(video_span, caches, norm_gains, shifts, weights, biases)
    return pl.pallas_call(
        hand_over,
        out_shape=(
            jax.ShapeDtypeStruct(video_span.shape, BF16),
            jax.ShapeDtypeStruct(caches.shape, BF16),
        ),
        in_specs=[anywhere, anywhere],
        out_specs=(anywhere, anywhere),
        scratch_shapes=[
            pltpu.VMEM(video_span.shape, BF16),
            pltpu.VMEM(caches.shape, BF16),
            dma(((1 + layers) * frames,)),
            dma(((1 + layers) * frames,)),
        ],
    )(encoded, carried)


def solution(mesh):
    return jax.shard_map(
        functools.partial(local, mesh.shape["lon"]),
        mesh=mesh,
        in_specs=(
            P(None, "clips", "lon", None),
            P(None, None, "clips", "lon", None),
            P(),
            P(),
            P(),
            P(),
        ),
        out_specs=(P(None, "clips", "lon", None), P(None, None, "clips", "lon", None)),
        check_vma=False,
    )
```

```python
import functools

import jax
import jax.numpy as jnp
from jax import lax
from jax.experimental import pallas as pl
from jax.experimental.pallas import tpu as pltpu
from jax.sharding import PartitionSpec as P

GROUPS = 32
EPSILON = 1e-06
MESH = pl.DeviceIdType.MESH
LO = 128
F32 = jnp.float32
BF16 = jnp.bfloat16


def kernel(
    peers,
    video_hbm, caches_hbm, gains_ref, shifts_ref, weights_hbm, biases_ref,
    encoded_hbm, carried_hbm,
    video, caches, raw, weights, x, cx, acc, edge_out, edge_in, cedge_out, cedge_in,
    hx, chx, jc, ja, stat_out, stat_in, params, carried, encoded,
    in_sem, w_sem, out_sem, stat_send, stat_recv, edge_send, edge_recv, cedge_send, cedge_recv,
):
    frames, height, width, channels = video.shape
    layers = caches.shape[0]
    half = height // 2
    rows = half * 16
    total = frames * rows
    hi_width = channels - LO
    lines = total // 8
    me = lax.axis_index("lon")
    right, left = lax.rem(me + 1, peers), lax.rem(me + peers - 1, peers)
    sides = (left, right)

    video_copy = pltpu.make_async_copy(video_hbm, video, in_sem.at[0])
    video_copy.start()
    cache_copies = [
        pltpu.make_async_copy(caches_hbm.at[l], caches.at[l], in_sem.at[1 + l]) for l in range(layers)
    ]
    cache_copies[0].start()

    weight_copies = [
        pltpu.make_async_copy(weights_hbm.at[l], raw.at[l], w_sem.at[l]) for l in range(layers)
    ]
    weight_copies[0].start()
    for l in range(1, layers):
        cache_copies[l].start()
        weight_copies[l].start()

    barrier = pltpu.get_barrier_semaphore()

    def greet(k, carry):
        pl.semaphore_signal(
            barrier, inc=1, device_id={"lon": lax.rem(me + k, peers)}, device_id_type=MESH
        )
        return carry

    lax.fori_loop(1, peers, greet, 0)

    params[...] = jnp.zeros_like(params)
    params[0:layers, 0:channels] = gains_ref[...]
    params[8 : 8 + layers, 0:channels] = shifts_ref[...]

    group_row = lax.broadcasted_iota(jnp.int32, (2 * LO, 2 * LO), 0) // (channels // GROUPS)
    group_column = lax.broadcasted_iota(jnp.int32, (2 * LO, 2 * LO), 1) // (channels // GROUPS)
    same_group = jnp.where(group_row == group_column, 1.0, 0.0).astype(BF16)

    lane8 = lax.broadcasted_iota(jnp.int32, (8, LO), 1)

    order = []
    for q in range(3):
        tap = [9 * q + 3 * r for r in range(3)]
        for r in range(3):
            order += [tap[r], tap[r] + 1]
        order += [tap[0] + 2, tap[1] + 2]
        if q != 1:
            order.append(tap[2] + 2)
        if q == 0:
            order.append(9 + 6 + 2)
    unit = LO // 2
    lane_w = lax.broadcasted_iota(jnp.int32, (channels, LO), 1)

    def arrange(l):
        def piece(u, upper):
            tile = raw[l, :, LO * (u // 2) : LO * (u // 2) + LO].astype(F32)
            return tile if u % 2 == upper else pltpu.roll(tile, unit, 1)

        for p in range(3):
            for d in range(0, 26, 2):
                a, b = 27 * p + order[d], 27 * p + order[d + 1]
                if a % 2 == 0 and b == a + 1:
                    weights[l, p, :, unit * d : unit * d + LO] = raw[l, :, unit * a : unit * a + LO]
                else:
                    both = jnp.where(lane_w < unit, piece(a, 0), piece(b, 1))
                    weights[l, p, :, unit * d : unit * d + LO] = both.astype(BF16)
            a = 27 * p + order[26]
            if a % 2 == 0:
                weights[l, p, :, unit * 26 : unit * 27] = raw[l, :, unit * a : unit * a + unit]
            else:
                weights[l, p, :, unit * 26 : unit * 27] = piece(a, 0)[:, 0:unit].astype(BF16)

    def spread(source, target):
        for f in range(frames):
            for hi in range(2):
                size = hi_width if hi else LO
                lanes = pl.ds(LO * hi, size)
                top = source[f, 0:half, :, lanes].astype(F32)
                bottom = source[f, half:height, :, lanes].astype(F32)
                both = jnp.concatenate([top, bottom], axis=1).reshape(rows, size)
                target[pl.ds(hi * total + f * rows, rows), 0:size] = both

    def take_edges(source, target):
        for hi in range(2):
            for side in range(2):
                column = source[pl.ds(hi * total + (width - 1) * side, lines, stride=8), :]
                target[side, hi, 0:lines, :] = column.astype(BF16)

    def edge_copies(source, target, send, recv, l):
        return [
            pltpu.make_async_remote_copy(
                src_ref=source.at[l, side],
                dst_ref=target.at[l, 1 - side],
                send_sem=send.at[l, side],
                recv_sem=recv.at[l, 1 - side],
                device_id={"lon": sides[side]},
                device_id_type=MESH,
            )
            for side in range(2)
        ]

    def local_stats(l):
        parts = []
        for hi in range(2):
            v = x[pl.ds(hi * total, total), :].reshape(lines, 8, LO)
            sums = (jnp.sum(v, axis=0), jnp.sum(v * v, axis=0))
            if hi:
                sums = tuple(jnp.where(lane8 < hi_width, t, 0.0) for t in sums)
            parts.append(sums)
        out = [
            jnp.sum(p, axis=0, keepdims=True)
            for p in (parts[0][0], parts[1][0], parts[0][1], parts[1][1])
        ]
        stat = jnp.concatenate(out + [jnp.zeros((4, LO), F32)], axis=0)
        stat_out[l] = stat
        stat_in[l, peers - 1] = stat

    def send_stats(l):
        def send(k, carry):
            pltpu.make_async_remote_copy(
                src_ref=stat_out.at[l],
                dst_ref=stat_in.at[l, k - 1],
                send_sem=stat_send.at[l],
                recv_sem=stat_recv.at[l],
                device_id={"lon": lax.rem(me + k, peers)},
                device_id_type=MESH,
            ).start()
            return carry

        lax.fori_loop(1, peers, send, 0)

    def stats_wait(sem, l):
        others = stat_in.at[l, pl.ds(0, peers - 1)]
        pltpu.make_async_copy(others, others, sem.at[l]).wait()

    def norm_terms(l):
        sums = jnp.sum(stat_in[l], axis=0)
        wide = jnp.concatenate(
            [
                jnp.concatenate([sums[0:1], sums[1:2]], axis=1),
                jnp.concatenate([sums[2:3], sums[3:4]], axis=1),
                jnp.zeros((6, 2 * LO), F32),
            ],
            axis=0,
        )
        first = wide.astype(BF16).astype(F32)
        second = (wide - first).astype(BF16).astype(F32)
        third = wide - first - second
        pieces = jnp.concatenate([third, second, first], axis=0).astype(BF16)
        grouped = jnp.dot(pieces, same_group, preferred_element_type=F32)
        grouped = grouped[0:8] + grouped[8:16] + grouped[16:24]
        entries = total * peers * (channels // GROUPS)
        average = grouped[0:1] / entries
        variance = jnp.maximum(grouped[1:2] / entries - average * average, 0.0)
        scale = lax.rsqrt(variance + EPSILON) * params[l : l + 1, :] * 0.5
        shift = params[8 + l : 9 + l, :] * 0.5
        return [
            tuple(t[:, LO * hi : LO * hi + LO] for t in (average, scale, shift)) for hi in range(2)
        ]

    def activate(v, terms):
        average, scale, shift = terms
        h = (v - average) * scale + shift
        return h + h * jnp.tanh(h)

    def place_edges(source, target, terms):
        for side in range(2):
            for hi in range(2):
                v = source[side, hi, 0:lines, :].astype(F32)
                if terms is not None:
                    v = activate(v, terms[hi])
                target[side, pl.ds(hi * total + (width - 1) * side, lines, stride=8), :] = v

    steps = 5 if half % 5 == 0 else 1
    size_i = half // steps
    block = size_i * 16
    column = lax.broadcasted_iota(jnp.int32, (2 * size_i, 8, LO), 1)
    lane = lax.broadcasted_iota(jnp.int32, (block, LO), 1)
    lane16 = lax.broadcasted_iota(jnp.int32, (16, LO), 1)

    def swap(v):
        return pltpu.roll(v, LO // 2, 1)

    def build(source, halo, target, terms, store, only):
        for f in only:

            def step(s, following):
                c = steps - 1 - s
                base = f * rows + c * block
                at = pl.ds(16 + c * block, block)
                wide = []
                for hi in range(2):
                    here = pl.ds(hi * total + base, block)
                    v = source[here, :]
                    if terms is not None:
                        v = activate(v, terms[hi])
                    v3 = v.reshape(2 * size_i, 8, LO)
                    before = jnp.where(
                        column == 0,
                        halo[0, here, :].reshape(2 * size_i, 8, LO),
                        pltpu.roll(v3, 1, 1),
                    ).reshape(block, LO)
                    after = jnp.where(
                        column == width - 1,
                        halo[1, here, :].reshape(2 * size_i, 8, LO),
                        pltpu.roll(v3, width - 1, 1),
                    ).reshape(block, LO)
                    wide.append((before, v, after))
                    if store is not None:
                        size = hi_width if hi else LO
                        pair = v.reshape(size_i, 16, LO)
                        for h in range(2):
                            store[
                                f, pl.ds(h * half + c * size_i, size_i), :, LO * hi : LO * hi + size
                            ] = pair[:, 8 * h : 8 * h + 8, 0:size].astype(BF16)
                for r in range(3):
                    target[f, at, LO * r : LO * r + LO] = wide[0][r].astype(BF16)
                before, middle, after = wide[1]
                target[f, at, 384:512] = jnp.where(lane < LO // 2, before, swap(middle)).astype(BF16)
                if block > 16:
                    nexts = jnp.concatenate([after[16:], following], axis=0)
                else:
                    nexts = following
                target[f, at, 512:640] = jnp.where(lane < LO // 2, after, swap(nexts)).astype(BF16)
                return after[0:16]

            following = jnp.zeros((16, LO), F32)
            for s in range(steps):
                following = step(s, following)
            zeros = jnp.zeros((8, 640), F32)
            first = target[f, 16:32, :].astype(F32)
            last = target[f, rows : rows + 16, :].astype(F32)
            over = jnp.concatenate([zeros, last[0:8]], axis=0)
            under = jnp.concatenate([first[8:16], zeros], axis=0)
            target[f, rows + 16 : rows + 32, :] = under.astype(BF16)
            target[f, 0:16, 0:512] = over[:, 0:512].astype(BF16)
            target[f, 0:16, 512:640] = jnp.where(
                lane16 < LO // 2, over[:, 512:640], swap(first[:, 512:640])
            ).astype(BF16)
            target[f, rows : rows + 16, 512:640] = jnp.where(
                lane16 < LO // 2, last[:, 512:640], swap(under[:, 512:640])
            ).astype(BF16)

    def conv(source, f, l, p):
        taps = jnp.concatenate(
            [
                source[f, 0:rows, 0:640],
                source[f, 16 : 16 + rows, 0:512],
                source[f, 32 : 32 + rows, 0:576],
            ],
            axis=1,
        )
        return lax.dot_general(
            taps, weights[l, p], (((1,), (1,)), ((), ())), preferred_element_type=F32
        )

    video_copy.wait()
    spread(video, x)
    local_stats(0)
    take_edges(x, edge_out.at[0])
    pl.semaphore_wait(barrier, peers - 1)
    pending = []
    send_stats(0)
    halo = edge_copies(edge_out, edge_in, edge_send, edge_recv, 0)
    for copy in halo:
        copy.start()

    cache_halos = []

    def send_cache(l):
        cache_copies[l].wait()
        spread(caches.at[l], cx.at[l])
        take_edges(cx.at[l], cedge_out.at[l])
        copies = edge_copies(cedge_out, cedge_in, cedge_send, cedge_recv, l)
        for copy in copies:
            copy.start()
        cache_halos.append(copies)

    def build_cache(l):
        for copy in cache_halos[l]:
            copy.wait()
        place_edges(cedge_in.at[l], chx, None)
        build(cx.at[l], chx, jc, None, None, range(frames))

    for l in range(layers):
        send_cache(l)
    weight_copies[0].wait()
    arrange(0)
    build_cache(0)

    for l in range(layers):
        bias = biases_ref[l : l + 1, :]
        acc[0:rows, :] = conv(jc, 0, l, 0) + bias
        acc[0:rows, :] += conv(jc, 1, l, 1)
        acc[rows:total, :] = conv(jc, 1, l, 0) + bias
        stats_wait(stat_recv, l)
        terms = norm_terms(l)
        for copy in halo:
            copy.wait()
        place_edges(edge_in.at[l], hx, terms)
        if l + 1 < layers:
            for copy in cache_halos[l + 1]:
                copy.wait()
            weight_copies[l + 1].wait()
        build(x, hx, ja, terms, carried.at[l], (0,))
        acc[0:rows, :] += conv(ja, 0, l, 2)
        build(x, hx, ja, terms, carried.at[l], (1,))
        acc[rows:total, :] += conv(ja, 0, l, 1)
        if l + 1 < layers:
            place_edges(cedge_in.at[l + 1], chx, None)
            build(cx.at[l + 1], chx, jc, None, None, range(frames))
            arrange(l + 1)
        acc[rows:total, :] += conv(ja, 1, l, 2)
        out = pltpu.make_async_copy(carried.at[l], carried_hbm.at[l], out_sem.at[l])
        out.start()
        pending.append(out)
        if l == 0:
            for hi in range(2):
                size = hi_width if hi else LO
                x[pl.ds(hi * total, total), 0:size] = acc[:, LO * hi : LO * hi + size]
        elif l == 1:
            spread(video, x)
            for hi in range(2):
                size = hi_width if hi else LO
                x[pl.ds(hi * total, total), 0:size] += acc[:, LO * hi : LO * hi + size]
        else:
            for f in range(frames):
                for hi in range(2):
                    size = hi_width if hi else LO
                    v = (
                        x[pl.ds(hi * total + f * rows, rows), 0:size]
                        + acc[f * rows : f * rows + rows, LO * hi : LO * hi + size]
                    ).reshape(half, 16, size)
                    for h in range(2):
                        encoded[
                            f, h * half : h * half + half, :, LO * hi : LO * hi + size
                        ] = v[:, 8 * h : 8 * h + 8, :].astype(BF16)
        if l + 1 < layers:
            local_stats(l + 1)
            send_stats(l + 1)
            take_edges(x, edge_out.at[l + 1])
            halo = edge_copies(edge_out, edge_in, edge_send, edge_recv, l + 1)
            for copy in halo:
                copy.start()
    out = pltpu.make_async_copy(encoded, encoded_hbm, out_sem.at[layers])
    out.start()
    pending.append(out)
    for l in range(layers):
        stats_wait(stat_send, l)
    for copy in pending:
        copy.wait()


def hand_over(encoded, carried, encoded_out, carried_out, held, held_all, in_sem, out_sem):
    layers, frames = carried.shape[:2]
    parts = []
    for f in range(frames):
        parts.append((encoded.at[f], held.at[f], encoded_out.at[f]))
        for l in range(layers):
            parts.append((carried.at[l, f], held_all.at[l, f], carried_out.at[l, f]))
    ins = [pltpu.make_async_copy(a, b, in_sem.at[i]) for i, (a, b, _) in enumerate(parts)]
    outs = [pltpu.make_async_copy(b, c, out_sem.at[i]) for i, (_, b, c) in enumerate(parts)]
    for copy in ins:
        copy.start()
    for arrive, leave in zip(ins, outs):
        arrive.wait()
        leave.start()
    for copy in outs:
        copy.wait()


def local(peers, video_span, caches, norm_gains, shifts, weights, biases):
    frames, height, width, channels = video_span.shape
    layers = caches.shape[0]
    weights = jnp.swapaxes(weights, 1, 2)
    rows = height * 8
    total = frames * rows
    lines = -(-(total // 8) // 16) * 16
    anywhere = pl.BlockSpec(memory_space=pl.ANY)
    vmem = pl.BlockSpec(memory_space=pltpu.VMEM)
    dma = pltpu.SemaphoreType.DMA
    flops = 2 * total * 27 * channels * channels * layers
    encoded, carried = pl.pallas_call(
        functools.partial(kernel, peers),
        out_shape=(
            jax.ShapeDtypeStruct(video_span.shape, BF16),
            jax.ShapeDtypeStruct(caches.shape, BF16),
        ),
        in_specs=[anywhere, anywhere, vmem, vmem, anywhere, vmem],
        out_specs=(anywhere, anywhere),
        scratch_shapes=[
            pltpu.VMEM(video_span.shape, BF16),
            pltpu.VMEM(caches.shape, BF16),
            pltpu.VMEM((layers, channels, 27 * channels), BF16),
            pltpu.VMEM((layers, 3, channels, 9 * channels), BF16),
            pltpu.VMEM((2 * total, LO), F32),
            pltpu.VMEM((layers, 2 * total, LO), F32),
            pltpu.VMEM((total, channels), F32),
            pltpu.VMEM((layers, 2, 2, lines, LO), BF16),
            pltpu.VMEM((layers, 2, 2, lines, LO), BF16),
            pltpu.VMEM((layers, 2, 2, lines, LO), BF16),
            pltpu.VMEM((layers, 2, 2, lines, LO), BF16),
            pltpu.VMEM((2, 2 * total, LO), F32),
            pltpu.VMEM((2, 2 * total, LO), F32),
            pltpu.VMEM((frames, rows + 32, 640), BF16),
            pltpu.VMEM((frames, rows + 32, 640), BF16),
            pltpu.VMEM((layers, 8, LO), F32),
            pltpu.VMEM((layers, peers, 8, LO), F32),
            pltpu.VMEM((16, 2 * LO), F32),
            pltpu.VMEM(caches.shape, BF16),
            pltpu.VMEM(video_span.shape, BF16),
            dma((1 + layers,)),
            dma((layers,)),
            dma((1 + layers,)),
            dma((layers,)),
            dma((layers,)),
            dma((layers, 2)),
            dma((layers, 2)),
            dma((layers, 2)),
            dma((layers, 2)),
        ],
        compiler_params=pltpu.CompilerParams(
            collective_id=0, has_side_effects=True, vmem_limit_bytes=56 * 2**20
        ),
        cost_estimate=pl.CostEstimate(
            flops=flops, bytes_accessed=20 * 2**20, transcendentals=layers * total * channels
        ),
    )(video_span, caches, norm_gains, shifts, weights, biases)
    return pl.pallas_call(
        hand_over,
        out_shape=(
            jax.ShapeDtypeStruct(video_span.shape, BF16),
            jax.ShapeDtypeStruct(caches.shape, BF16),
        ),
        in_specs=[anywhere, anywhere],
        out_specs=(anywhere, anywhere),
        scratch_shapes=[
            pltpu.VMEM(video_span.shape, BF16),
            pltpu.VMEM(caches.shape, BF16),
            dma(((1 + layers) * frames,)),
            dma(((1 + layers) * frames,)),
        ],
    )(encoded, carried)


def solution(mesh):
    return jax.shard_map(
        functools.partial(local, mesh.shape["lon"]),
        mesh=mesh,
        in_specs=(
            P(None, "clips", "lon", None),
            P(None, None, "clips", "lon", None),
            P(),
            P(),
            P(),
            P(),
        ),
        out_specs=(P(None, "clips", "lon", None), P(None, None, "clips", "lon", None)),
        check_vma=False,
    )
```
